32 devices in a mesh: blk: 8 (over y, x, core), tm: 4 (over z).
Axes of the slice: x: 2, y: 2, z: 4, core: 2. Of those that a mesh axis runs over, the one named last changes fastest.
Arguments:
- records: bfloat16 [2048, 16, 512], P('blk', 'tm'), may hold values from -6 to 6
- glitch_mask: int32 [2048, 16], P('blk'), may hold values 0 or 1
- fir_taps: bfloat16 [65], replicated, may hold values from -1.1953125 to 1.1953125
Outputs:
- correlations: bfloat16 [16, 2048, 2048], P('tm', 'blk')
The draws below stay inside these ranges and needn't reach their ends.
All inputs are finite; a program needn't handle non-finite values. No bound on the sum of `glitch_mask` on one device may be relied on, other than what follows from the above.
Results may differ from the reference program's by a relative error of at most 0.015.
Values may be sent and summed in bfloat16 or wider, within the bound.
A program may use at most 256 MiB of HBM per device.

```python
import math
import jax
import jax.numpy as jnp
from jax import lax

SEGLEN = 512
BINS = 128
FIRST_BIN = 16
TAPS = 65
SMOOTH = 64
LAGS = 16
BLOCK_CH = 256
CHANNELS = 2048
SEGMENTS = 16
N_BLK = 8
N_TM = 4


def touch_ends(result, rng, least, high):
    index_at = [jax.random.randint(jax.random.fold_in(rng, axis), (), 0, length) for axis, length in enumerate(result.shape)]
    widest = result.shape.index(max(result.shape))
    beside = index_at[:widest] + [(index_at[widest] + 1) % result.shape[widest]] + index_at[widest + 1:]
    return result.at[tuple(index_at)].set(least).at[tuple(beside)].set(high)


def level_of(rng, extent, shards, least, high):
    loudness, own = 1.0, jax.random.fold_in(rng, 6)
    for axis_at, shards_of in shards:
        steps = jnp.exp(jax.random.uniform(jax.random.fold_in(own, axis_at), (shards_of,), jnp.float32, least / len(shards), high / len(shards)))
        loudness = loudness * jnp.repeat(steps, extent[axis_at] // shards_of).reshape([-1 if axis == axis_at else 1 for axis in range(len(extent))])
    return loudness


def bell_draw(rng, shape, scale, bound, shards=(), kind=jnp.bfloat16):
    result = scale * jax.random.normal(rng, shape, jnp.float32)
    if shards:
        result = result * level_of(rng, shape, shards, -0.22, 0.18)
    return jnp.clip(result, -bound, bound).astype(kind)


def setup_inputs(seed: int = 0) -> dict:
    arg_keys = jax.random.split(jax.random.key(seed), 4)
    return {
        "records": bell_draw(arg_keys[0], (CHANNELS, SEGMENTS, SEGLEN), 1.0, 6.0, ((0, 8), (1, 4))),
        "glitch_mask": touch_ends((jax.random.randint(arg_keys[1], (CHANNELS, SEGMENTS), 0, 5) < 4).astype(jnp.int32), jax.random.fold_in(arg_keys[1], 1), 0, 1),
        "fir_taps": bell_draw(arg_keys[2], (TAPS,), 0.2, 1.1953125),
    }


def filter_matrix(fir_taps):
    source = lax.broadcasted_iota(jnp.int32, (SEGLEN, SEGLEN), 0)
    target = lax.broadcasted_iota(jnp.int32, (SEGLEN, SEGLEN), 1)
    offsets = source - target + (TAPS - 1) // 2
    weights = fir_taps.astype(jnp.float32)
    matrix = jnp.zeros((SEGLEN, SEGLEN), jnp.float32)
    for tap_index in range(TAPS):
        matrix = matrix + jnp.where(offsets == tap_index, weights[tap_index], jnp.float32(0.0))
    return matrix

def transform_table(fir_taps):
    sample = lax.broadcasted_iota(jnp.int32, (SEGLEN, BINS), 0)
    freq = lax.broadcasted_iota(jnp.int32, (SEGLEN, BINS), 1) + FIRST_BIN
    phase = sample * freq % SEGLEN
    angle = phase.astype(jnp.float32) * jnp.float32(2.0 * math.pi / SEGLEN)
    dft = jnp.concatenate([jnp.cos(angle), -jnp.sin(angle)], axis=1)
    combined = jnp.dot(filter_matrix(fir_taps), dft, precision=lax.Precision.HIGHEST, preferred_element_type=jnp.float32)
    return combined.astype(jnp.bfloat16)

def smoothing():
    source = lax.broadcasted_iota(jnp.int32, (SEGLEN, SEGLEN), 0)
    target = lax.broadcasted_iota(jnp.int32, (SEGLEN, SEGLEN), 1)
    inside = jnp.abs(source - target) <= SMOOTH
    band_ones = jnp.where(inside, 1.0, 0.0).astype(jnp.bfloat16)
    counts = lax.optimization_barrier(jnp.sum(jnp.where(inside, 1.0, 0.0).astype(jnp.float32), axis=0))
    return (band_ones, counts)

def whiten(samples, usable, combined, band_ones, counts):
    envelope = jnp.dot(jnp.abs(samples), band_ones, preferred_element_type=jnp.float32) / counts[None, :]
    normal = (samples.astype(jnp.float32) / (envelope + 1e-06)).astype(jnp.bfloat16)
    spectra = jnp.dot(normal, combined, preferred_element_type=jnp.float32)
    real_part = spectra[:, :BINS]
    imag_part = spectra[:, BINS:]
    power_mean = lax.optimization_barrier(jnp.mean(real_part * real_part + imag_part * imag_part, axis=1, keepdims=True))
    scale_rows = usable.astype(jnp.float32)[:, None] / jnp.sqrt(power_mean + 1e-06)
    return (spectra * scale_rows).astype(jnp.bfloat16)

def lag_tables():
    delay = lax.broadcasted_iota(jnp.int32, (LAGS, BINS), 0) - LAGS // 2
    freq = lax.broadcasted_iota(jnp.int32, (LAGS, BINS), 1) + FIRST_BIN
    phase = delay * freq % SEGLEN
    angle = phase.astype(jnp.float32) * jnp.float32(2.0 * math.pi / SEGLEN)
    factor = jnp.float32(1.0 / math.sqrt(SEGMENTS * BINS))
    return ((jnp.cos(angle) * factor).astype(jnp.bfloat16), (jnp.sin(angle) * factor).astype(jnp.bfloat16))

def reference(records, glitch_mask, fir_taps):
    combined = transform_table(fir_taps)
    band_ones, counts = smoothing()
    rows_block = BLOCK_CH * SEGMENTS
    blocks = records.reshape(N_BLK, rows_block, SEGLEN)
    masks = glitch_mask.reshape(N_BLK, rows_block)
    whitened = lax.map(lambda pair: whiten(pair[0], pair[1], combined, band_ones, counts), (blocks, masks))
    spectra = whitened.reshape(CHANNELS, SEGMENTS, 2, BINS).astype(jnp.float32)
    real_all = jnp.transpose(spectra[:, :, 0, :], (2, 1, 0))
    imag_all = jnp.transpose(spectra[:, :, 1, :], (2, 1, 0))
    cos_rows, sin_rows = lag_tables()
    band_bins = BINS // N_TM
    cos_bands = cos_rows.astype(jnp.float32).reshape(LAGS, N_TM, band_bins)
    sin_bands = sin_rows.astype(jnp.float32).reshape(LAGS, N_TM, band_bins)

    def column_block(block_index):
        start = (block_index * BLOCK_CH).astype(jnp.int32)
        other_real = lax.dynamic_slice_in_dim(real_all, start, BLOCK_CH, 2)
        other_imag = lax.dynamic_slice_in_dim(imag_all, start, BLOCK_CH, 2)
        cross_real = jnp.einsum('fsi,fsj->fij', real_all, other_real) + jnp.einsum('fsi,fsj->fij', imag_all, other_imag)
        cross_imag = jnp.einsum('fsi,fsj->fij', imag_all, other_real) - jnp.einsum('fsi,fsj->fij', real_all, other_imag)
        cross_real = lax.optimization_barrier(cross_real.astype(jnp.bfloat16)).astype(jnp.float32)
        cross_imag = lax.optimization_barrier(cross_imag.astype(jnp.bfloat16)).astype(jnp.float32)
        cross_real = cross_real.reshape(N_TM, band_bins, CHANNELS, BLOCK_CH)
        cross_imag = cross_imag.reshape(N_TM, band_bins, CHANNELS, BLOCK_CH)
        partial_terms = jnp.einsum('ltf,tfij->tlij', cos_bands, cross_real) - jnp.einsum('ltf,tfij->tlij', sin_bands, cross_imag)
        partial_terms = lax.optimization_barrier(partial_terms.astype(jnp.bfloat16)).astype(jnp.float32)
        return lax.optimization_barrier(jnp.sum(partial_terms, axis=0)).astype(jnp.bfloat16)
    columns = lax.map(column_block, jnp.arange(N_BLK, dtype=jnp.int32))
    return jnp.transpose(columns, (1, 2, 0, 3)).reshape(LAGS, CHANNELS, CHANNELS)
```

```python
import math

import jax
import jax.numpy as jnp
import numpy as np
from jax import lax
from jax.sharding import PartitionSpec as P

BINS = 128
FIRST_BIN = 16
SMOOTH = 64
LAGS = 16


def dft_thirds(seglen):
    sample = np.arange(seglen)[:, None]
    freq = np.arange(BINS)[None, :] + FIRST_BIN
    angle = (sample * freq % seglen) * (2.0 * math.pi / seglen)
    rest = np.concatenate([np.cos(angle), -np.sin(angle)], axis=1).astype(np.float32)
    thirds = []
    for _ in range(3):
        part = rest.astype(jnp.bfloat16)
        thirds.append(part)
        rest = rest - part.astype(np.float32)
    return np.concatenate(thirds, axis=1)


def lag_rows(seg_total, seglen):
    delay = np.arange(LAGS)[:, None] - LAGS // 2
    freq = np.arange(BINS)[None, :] + FIRST_BIN
    angle = (delay * freq % seglen) * (2.0 * math.pi / seglen)
    factor = 1.0 / math.sqrt(seg_total * BINS)
    tables = np.stack([np.cos(angle), np.sin(angle)]).astype(np.float32) * np.float32(factor)
    return tables.astype(jnp.bfloat16).astype(np.float32)


def filter_matrix(fir_taps, seglen):
    half = (fir_taps.shape[0] - 1) // 2
    period = 2 * seglen
    line = jnp.pad(fir_taps[::-1], (seglen - 1 - half, seglen - half))
    rows = jnp.tile(line, seglen)[: seglen * (period - 1)].reshape(seglen, period - 1)
    return rows[:, seglen - 1 :]


def transform_table(fir_taps, seglen):
    parts = jnp.dot(
        filter_matrix(fir_taps, seglen),
        jnp.asarray(dft_thirds(seglen)),
        preferred_element_type=jnp.float32,
    )
    width = 2 * BINS
    total = parts[:, :width] + (parts[:, width : 2 * width] + parts[:, 2 * width :])
    return total.astype(jnp.bfloat16)


def whiten(samples, usable, fir_taps):
    seglen = samples.shape[1]
    source = lax.broadcasted_iota(jnp.int32, (seglen, seglen), 0)
    target = lax.broadcasted_iota(jnp.int32, (seglen, seglen), 1)
    band_ones = jnp.where(jnp.abs(source - target) <= SMOOTH, 1.0, 0.0).astype(jnp.bfloat16)
    where = lax.broadcasted_iota(jnp.int32, (1, seglen), 1)
    counts = jnp.minimum(where, SMOOTH) + jnp.minimum(seglen - 1 - where, SMOOTH) + 1
    envelope = jnp.dot(
        jnp.abs(samples), band_ones, preferred_element_type=jnp.float32
    ) / counts.astype(jnp.float32)
    normal = (samples.astype(jnp.float32) / (envelope + 1e-06)).astype(jnp.bfloat16)
    spectra = jnp.dot(normal, transform_table(fir_taps, seglen), preferred_element_type=jnp.float32)
    power = jnp.sum(spectra * spectra, axis=1, keepdims=True) * jnp.float32(1.0 / BINS)
    scale = usable.astype(jnp.float32)[:, None] / jnp.sqrt(power + 1e-06)
    return (spectra * scale).astype(jnp.bfloat16)


def body(records, glitch_mask, fir_taps):
    tm_count = lax.axis_size("tm")
    tm_index = lax.axis_index("tm")
    chans, segs, seglen = records.shape
    seg_total = glitch_mask.shape[1]
    usable = lax.dynamic_slice_in_dim(glitch_mask, tm_index * segs, segs, 1)
    white = whiten(records.reshape(chans * segs, seglen), usable.reshape(chans * segs), fir_taps)
    slab = white.reshape(chans, segs * 2 * BINS)
    column = lax.all_gather(slab, "tm", axis=1, tiled=True)
    every = lax.all_gather(column, "blk", axis=0, tiled=True)
    lags_dev = LAGS // tm_count
    tables = lax.dynamic_slice_in_dim(
        jnp.asarray(lag_rows(seg_total, seglen)), tm_index * lags_dev, lags_dev, 1
    )
    cos_rows = tables[0][:, None, None, :]
    sin_rows = tables[1][:, None, None, :]
    own = column.reshape(chans, seg_total, 2, BINS).astype(jnp.float32)
    real_part, imag_part = own[None, :, :, 0], own[None, :, :, 1]
    turned = jnp.stack(
        [cos_rows * real_part - sin_rows * imag_part, cos_rows * imag_part + sin_rows * real_part],
        axis=3,
    ).astype(jnp.bfloat16)
    left = turned.reshape(lags_dev, chans, seg_total * 2 * BINS)
    return jnp.einsum("lik,jk->lij", left, every, preferred_element_type=jnp.float32).astype(
        jnp.bfloat16
    )


def solution(mesh):
    placed = (P("blk", "tm", None), P("blk", None), P())
    return jax.shard_map(
        body, mesh=mesh, in_specs=placed, out_specs=P("tm", "blk", None), check_vma=False
    )
```

```python
import math

import jax
import jax.numpy as jnp
import numpy as np
from jax import lax
from jax.experimental import pallas as pl
from jax.experimental.pallas import tpu as pltpu
from jax.sharding import PartitionSpec as P

BINS = 128
FIRST_BIN = 16
SMOOTH = 64
LAGS = 16


def dft_thirds(seglen):
    sample = np.arange(seglen)[:, None]
    freq = np.arange(BINS)[None, :] + FIRST_BIN
    angle = (sample * freq % seglen) * (2.0 * math.pi / seglen)
    rest = np.concatenate([np.cos(angle), -np.sin(angle)], axis=1).astype(np.float32)
    thirds = []
    for _ in range(3):
        part = rest.astype(jnp.bfloat16)
        thirds.append(part)
        rest = rest - part.astype(np.float32)
    return np.concatenate(thirds, axis=1)


def lag_rows(seg_total, seglen):
    delay = np.arange(LAGS)[:, None] - LAGS // 2
    freq = np.arange(BINS)[None, :] + FIRST_BIN
    angle = (delay * freq % seglen) * (2.0 * math.pi / seglen)
    factor = 1.0 / math.sqrt(seg_total * BINS)
    tables = np.stack([np.cos(angle), np.sin(angle)]).astype(np.float32) * np.float32(factor)
    return tables.astype(jnp.bfloat16).astype(np.float32)


def filter_matrix(fir_taps, seglen):
    half = (fir_taps.shape[0] - 1) // 2
    period = 2 * seglen
    line = jnp.pad(fir_taps[::-1], (seglen - 1 - half, seglen - half))
    rows = jnp.tile(line, seglen)[: seglen * (period - 1)].reshape(seglen, period - 1)
    return rows[:, seglen - 1 :]


def transform_table(fir_taps, seglen):
    parts = jnp.dot(
        filter_matrix(fir_taps, seglen),
        jnp.asarray(dft_thirds(seglen)),
        preferred_element_type=jnp.float32,
    )
    width = 2 * BINS
    total = parts[:, :width] + (parts[:, width : 2 * width] + parts[:, 2 * width :])
    return total.astype(jnp.bfloat16)


def whiten(samples, usable, fir_taps):
    seglen = samples.shape[1]
    source = lax.broadcasted_iota(jnp.int32, (seglen, seglen), 0)
    target = lax.broadcasted_iota(jnp.int32, (seglen, seglen), 1)
    band_ones = jnp.where(jnp.abs(source - target) <= SMOOTH, 1.0, 0.0).astype(jnp.bfloat16)
    where = lax.broadcasted_iota(jnp.int32, (1, seglen), 1)
    counts = jnp.minimum(where, SMOOTH) + jnp.minimum(seglen - 1 - where, SMOOTH) + 1
    envelope = jnp.dot(
        jnp.abs(samples), band_ones, preferred_element_type=jnp.float32
    ) / counts.astype(jnp.float32)
    normal = (samples.astype(jnp.float32) / (envelope + 1e-06)).astype(jnp.bfloat16)
    spectra = jnp.dot(normal, transform_table(fir_taps, seglen), preferred_element_type=jnp.float32)
    power = jnp.sum(spectra * spectra, axis=1, keepdims=True) * jnp.float32(1.0 / BINS)
    scale = usable.astype(jnp.float32)[:, None] / jnp.sqrt(power + 1e-06)
    return (spectra * scale).astype(jnp.bfloat16)


def gathered_body(records, glitch_mask, fir_taps):
    tm_count = lax.axis_size("tm")
    tm_index = lax.axis_index("tm")
    chans, segs, seglen = records.shape
    seg_total = glitch_mask.shape[1]
    usable = lax.dynamic_slice_in_dim(glitch_mask, tm_index * segs, segs, 1)
    white = whiten(records.reshape(chans * segs, seglen), usable.reshape(chans * segs), fir_taps)
    slab = white.reshape(chans, segs * 2 * BINS)
    column = lax.all_gather(slab, "tm", axis=1, tiled=True)
    every = lax.all_gather(column, "blk", axis=0, tiled=True)
    lags_dev = LAGS // tm_count
    tables = lax.dynamic_slice_in_dim(
        jnp.asarray(lag_rows(seg_total, seglen)), tm_index * lags_dev, lags_dev, 1
    )
    cos_rows = tables[0][:, None, None, :]
    sin_rows = tables[1][:, None, None, :]
    own = column.reshape(chans, seg_total, 2, BINS).astype(jnp.float32)
    real_part, imag_part = own[None, :, :, 0], own[None, :, :, 1]
    turned = jnp.stack(
        [cos_rows * real_part - sin_rows * imag_part, cos_rows * imag_part + sin_rows * real_part],
        axis=3,
    ).astype(jnp.bfloat16)
    left = turned.reshape(lags_dev, chans, seg_total * 2 * BINS)
    return jnp.einsum("lik,jk->lij", left, every, preferred_element_type=jnp.float32).astype(
        jnp.bfloat16
    )


NEAREST = ((0, 1, 2, 3), (1, 2, 0, 3), (2, 1, 3, 0), (3, 2, 1, 0))
MESH = pl.DeviceIdType.MESH


def kernel(x_ref, use_ref, line_ref, dft_ref, tab_ref, out_ref, slabs, left, acc, done, sent, got, outs):
    segs, chans, seglen = x_ref.shape
    width = 2 * BINS
    depth = segs * width
    lags = left.shape[1]
    half = chans // 2
    b, z = lax.axis_index("blk"), lax.axis_index("tm")
    core = lax.rem(b, 2)
    at_x = lax.rem(lax.div(b, 2), 2)
    at_y = lax.div(b, 4)
    sib = b + 1 - 2 * core
    by_x = b + 2 - 4 * at_x
    by_y = b + 4 - 8 * at_y
    across = by_x + 4 - 8 * at_y
    up, down = z + 1, z - 1
    has_up, has_down = z < 3, z > 0

    barrier = pltpu.get_barrier_semaphore()
    for peer in (sib, by_x, by_y):
        pl.semaphore_signal(barrier, inc=1, device_id=(peer, z), device_id_type=MESH)

    @pl.when(has_up)
    def _():
        pl.semaphore_signal(barrier, inc=1, device_id=(b, up), device_id_type=MESH)

    @pl.when(has_down)
    def _():
        pl.semaphore_signal(barrier, inc=1, device_id=(b, down), device_id_type=MESH)

    def slab_of(plane, block):
        return plane * 8 + block

    own = slab_of(z, b)
    line = jnp.broadcast_to(line_ref[...], (seglen, 2 * seglen))
    fir = pltpu.roll(line, 0, 1, stride=1, stride_axis=0)[:, :seglen].astype(jnp.bfloat16)
    parts = jnp.dot(fir, dft_ref[...], preferred_element_type=jnp.float32)
    table = (parts[:, :width] + (parts[:, width : 2 * width] + parts[:, 2 * width :])).astype(jnp.bfloat16)
    source = lax.broadcasted_iota(jnp.int32, (seglen, seglen), 0)
    target = lax.broadcasted_iota(jnp.int32, (seglen, seglen), 1)
    band_ones = jnp.where(jnp.abs(source - target) <= SMOOTH, 1.0, 0.0).astype(jnp.bfloat16)
    where = lax.broadcasted_iota(jnp.int32, (1, seglen), 1)
    counts = jnp.minimum(where, SMOOTH) + jnp.minimum(seglen - 1 - where, SMOOTH) + 1
    counts = counts.astype(jnp.float32)
    for s in range(segs):
        samples = x_ref[s]
        envelope = jnp.dot(jnp.abs(samples), band_ones, preferred_element_type=jnp.float32) / counts
        normal = (samples.astype(jnp.float32) / (envelope + 1e-06)).astype(jnp.bfloat16)
        spectra = jnp.dot(normal, table, preferred_element_type=jnp.float32)
        power = jnp.sum(spectra * spectra, axis=1, keepdims=True) * jnp.float32(1.0 / BINS)
        scale = use_ref[:, s : s + 1] / jnp.sqrt(power + 1e-06)
        slabs[own, :, s * width : (s + 1) * width] = (spectra * scale).astype(jnp.bfloat16)

    pl.semaphore_wait(barrier, 3 + has_up.astype(jnp.int32) + has_down.astype(jnp.int32))

    sends = []

    def view(slab, part):
        if part is None:
            return slabs.at[slab], got.at[slab, 0]
        return slabs.at[slab, pl.ds(part * half, half)], got.at[slab, part]

    def send(slab, block, plane, part=None, when=None):
        ref, sem = view(slab, part)
        copy = pltpu.make_async_remote_copy(
            src_ref=ref, dst_ref=ref, send_sem=sent.at[len(sends)], recv_sem=sem,
            device_id=(block, plane), device_id_type=MESH,
        )
        sends.append((copy, when))
        if when is None:
            copy.start()
        else:
            pl.when(when)(copy.start)

    def arrive(slab, part=None):
        ref, sem = view(slab, part)
        pltpu.make_async_remote_copy(
            src_ref=ref, dst_ref=ref, send_sem=sent.at[0], recv_sem=sem,
            device_id=(sib, z), device_id_type=MESH,
        ).wait_recv()

    plane_at, onward, goes_on = [z], [None], [None]
    for step in range(1, 4):
        plane = sum(jnp.where(z == at, NEAREST[at][step], 0) for at in range(4))
        following = jnp.where(plane > z, z - 1, z + 1)
        plane_at.append(plane)
        onward.append(following)
        goes_on.append(jnp.logical_and(following >= 0, following <= 3))

    def turn(step):
        slab = slab_of(plane_at[step], b)

        def one(lag, carry):
            row = z * lags + lag
            cos_row = tab_ref[0, pl.ds(row, 1), :]
            sin_row = tab_ref[1, pl.ds(row, 1), :]
            for s in range(segs):
                at = s * width
                real_part = slabs[slab, :, at : at + BINS].astype(jnp.float32)
                imag_part = slabs[slab, :, at + BINS : at + width].astype(jnp.float32)
                left[step, lag, :, at : at + BINS] = (
                    cos_row * real_part - sin_row * imag_part
                ).astype(jnp.bfloat16)
                left[step, lag, :, at + BINS : at + width] = (
                    cos_row * imag_part + sin_row * real_part
                ).astype(jnp.bfloat16)
            return carry

        lax.fori_loop(0, lags, one, 0)

    copies = []

    def correlate(step, block):
        pair = lax.div(block, 2)
        first_slab = slab_of(plane_at[step], pair * 2)
        columns = pl.ds(pl.multiple_of(pair * 2 * chans, 2 * chans), 2 * chans)

        def one(lag, carry):
            right = slabs[pl.ds(first_slab, 2)].reshape(2 * chans, depth)
            term = lax.dot_general(
                left[step, lag], right, (((1,), (1,)), ((), ())), preferred_element_type=jnp.float32
            )
            if step == 0:
                acc[lag, :, columns] = term
            elif step < 3:
                acc[lag, :, columns] += term
            else:
                done[lag, :, columns] = (acc[lag, :, columns] + term).astype(jnp.bfloat16)
            return carry

        lax.fori_loop(0, lags, one, 0)
        if step == 3:
            copy = pltpu.make_async_copy(
                done.at[:, :, columns], out_ref.at[:, :, columns], outs.at[len(copies)]
            )
            copy.start()
            copies.append(copy)

    def other_core(block):
        return block + 1 - 2 * core

    send(own, b, up, when=has_up)
    send(own, b, down, when=has_down)
    send(own, by_x, z)
    send(own, by_y, z)
    send(own, sib, z)
    turn(0)

    def corner(step):
        slab = slab_of(plane_at[step], across)
        if step in (0, 3):
            arrive(slab, 0)
            arrive(slab, 1)
        else:
            arrive(slab)
        if step == 0:
            send(slab, b, up, when=has_up)
            send(slab, b, down, when=has_down)
        elif step == 1:
            send(slab, b, onward[1], when=goes_on[1])
        send(slab, sib, z)
        arrive(slab_of(plane_at[step], other_core(across)))
        correlate(step, across)

    for step in range(4):
        plane = plane_at[step]
        if step < 3:
            slab = slab_of(plane_at[step + 1], b)
            arrive(slab)
            send(slab, b, onward[step + 1], when=goes_on[step + 1])
            send(slab, by_x, z)
            send(slab, by_y, z)
            send(slab, sib, z)
        slab = slab_of(plane, by_x)
        arrive(slab)
        if step in (0, 3):
            send(slab, by_y, z, part=0)
        send(slab, sib, z)
        slab = slab_of(plane, by_y)
        arrive(slab)
        if step in (0, 3):
            send(slab, by_x, z, part=1)
        send(slab, sib, z)
        for block in (b, by_x, by_y):
            arrive(slab_of(plane, other_core(block)))
            correlate(step, block)
        if step < 3:
            turn(step + 1)
        if step == 0:
            corner(0)
        elif step == 2:
            corner(1)
    corner(2)
    corner(3)

    for copy in copies:
        copy.wait()
    for copy, when in sends:
        if when is None:
            copy.wait_send()
        else:
            pl.when(when)(copy.wait_send)


def kernel_body(records, glitch_mask, fir_taps):
    blocks, planes = lax.axis_size("blk"), lax.axis_size("tm")
    tm_index = lax.axis_index("tm")
    chans, segs, seglen = records.shape
    seg_total = glitch_mask.shape[1]
    lags_dev = LAGS // planes
    depth = segs * 2 * BINS
    usable = lax.dynamic_slice_in_dim(glitch_mask, tm_index * segs, segs, 1).astype(jnp.float32)
    middle = (fir_taps.shape[0] - 1) // 2
    back = fir_taps[::-1].astype(jnp.float32)
    line = jnp.concatenate(
        [back[middle:], jnp.zeros((2 * seglen - 2 * middle - 1,), jnp.float32), back[:middle]]
    )[None, :]
    bf16 = jnp.bfloat16
    return pl.pallas_call(
        kernel,
        out_shape=jax.ShapeDtypeStruct((lags_dev, chans, chans * blocks), bf16),
        in_specs=[pl.BlockSpec(memory_space=pltpu.VMEM)] * 5,
        out_specs=pl.BlockSpec(memory_space=pl.ANY),
        scratch_shapes=[
            pltpu.VMEM((blocks * planes, chans, depth), bf16),
            pltpu.VMEM((planes, lags_dev, chans, depth), bf16),
            pltpu.VMEM((lags_dev, chans, chans * blocks), jnp.float32),
            pltpu.VMEM((lags_dev, chans, chans * blocks), bf16),
            pltpu.SemaphoreType.DMA((48,)),
            pltpu.SemaphoreType.DMA((blocks * planes, 2)),
            pltpu.SemaphoreType.DMA((4,)),
        ],
        compiler_params=pltpu.CompilerParams(
            collective_id=0, has_side_effects=True, vmem_limit_bytes=58 * 1024 * 1024
        ),
        cost_estimate=pl.CostEstimate(
            flops=2 * lags_dev * chans * chans * blocks * planes * depth,
            bytes_accessed=2 * lags_dev * chans * chans * blocks,
            transcendentals=0,
        ),
    )(
        jnp.transpose(records, (1, 0, 2)),
        usable,
        line,
        jnp.asarray(dft_thirds(seglen)),
        jnp.asarray(lag_rows(seg_total, seglen)),
    )


def solution(mesh):
    placed = (P("blk", "tm", None), P("blk", None), P())
    small = mesh.shape["blk"] == 8 and mesh.shape["tm"] == 4
    return jax.shard_map(
        kernel_body if small else gathered_body,
        mesh=mesh,
        in_specs=placed,
        out_specs=P("tm", "blk", None),
        check_vma=False,
    )
```

```python
import math

import jax
import jax.numpy as jnp
import numpy as np
from jax import lax
from jax.experimental import pallas as pl
from jax.experimental.pallas import tpu as pltpu
from jax.sharding import PartitionSpec as P

BINS = 128
FIRST_BIN = 16
SMOOTH = 64
LAGS = 16
GROUP = 4


def dft_thirds(seglen):
    sample = np.arange(seglen)[:, None]
    freq = np.arange(BINS)[None, :] + FIRST_BIN
    angle = (sample * freq % seglen) * (2.0 * math.pi / seglen)
    rest = np.concatenate([np.cos(angle), -np.sin(angle)], axis=1).astype(np.float32)
    thirds = []
    for _ in range(3):
        part = rest.astype(jnp.bfloat16)
        thirds.append(part)
        rest = rest - part.astype(np.float32)
    return np.concatenate(thirds, axis=1)


def lag_rows(seg_total, seglen):
    delay = np.arange(LAGS)[:, None] - LAGS // 2
    freq = np.arange(BINS)[None, :] + FIRST_BIN
    angle = (delay * freq % seglen) * (2.0 * math.pi / seglen)
    factor = 1.0 / math.sqrt(seg_total * BINS)
    tables = np.stack([np.cos(angle), np.sin(angle)]).astype(np.float32) * np.float32(factor)
    return tables.astype(jnp.bfloat16).astype(np.float32)


def filter_matrix(fir_taps, seglen):
    half = (fir_taps.shape[0] - 1) // 2
    period = 2 * seglen
    line = jnp.pad(fir_taps[::-1], (seglen - 1 - half, seglen - half))
    rows = jnp.tile(line, seglen)[: seglen * (period - 1)].reshape(seglen, period - 1)
    return rows[:, seglen - 1 :]


def transform_table(fir_taps, seglen):
    parts = jnp.dot(
        filter_matrix(fir_taps, seglen),
        jnp.asarray(dft_thirds(seglen)),
        preferred_element_type=jnp.float32,
    )
    width = 2 * BINS
    total = parts[:, :width] + (parts[:, width : 2 * width] + parts[:, 2 * width :])
    return total.astype(jnp.bfloat16)


def whiten(samples, usable, fir_taps):
    seglen = samples.shape[1]
    source = lax.broadcasted_iota(jnp.int32, (seglen, seglen), 0)
    target = lax.broadcasted_iota(jnp.int32, (seglen, seglen), 1)
    band_ones = jnp.where(jnp.abs(source - target) <= SMOOTH, 1.0, 0.0).astype(jnp.bfloat16)
    where = lax.broadcasted_iota(jnp.int32, (1, seglen), 1)
    counts = jnp.minimum(where, SMOOTH) + jnp.minimum(seglen - 1 - where, SMOOTH) + 1
    envelope = jnp.dot(
        jnp.abs(samples), band_ones, preferred_element_type=jnp.float32
    ) / counts.astype(jnp.float32)
    normal = (samples.astype(jnp.float32) / (envelope + 1e-06)).astype(jnp.bfloat16)
    spectra = jnp.dot(normal, transform_table(fir_taps, seglen), preferred_element_type=jnp.float32)
    power = jnp.sum(spectra * spectra, axis=1, keepdims=True) * jnp.float32(1.0 / BINS)
    scale = usable.astype(jnp.float32)[:, None] / jnp.sqrt(power + 1e-06)
    return (spectra * scale).astype(jnp.bfloat16)


def gathered_body(records, glitch_mask, fir_taps):
    tm_count = lax.axis_size("tm")
    tm_index = lax.axis_index("tm")
    chans, segs, seglen = records.shape
    seg_total = glitch_mask.shape[1]
    usable = lax.dynamic_slice_in_dim(glitch_mask, tm_index * segs, segs, 1)
    white = whiten(records.reshape(chans * segs, seglen), usable.reshape(chans * segs), fir_taps)
    slab = white.reshape(chans, segs * 2 * BINS)
    column = lax.all_gather(slab, "tm", axis=1, tiled=True)
    every = lax.all_gather(column, "blk", axis=0, tiled=True)
    lags_dev = LAGS // tm_count
    tables = lax.dynamic_slice_in_dim(
        jnp.asarray(lag_rows(seg_total, seglen)), tm_index * lags_dev, lags_dev, 1
    )
    cos_rows = tables[0][:, None, None, :]
    sin_rows = tables[1][:, None, None, :]
    own = column.reshape(chans, seg_total, 2, BINS).astype(jnp.float32)
    real_part, imag_part = own[None, :, :, 0], own[None, :, :, 1]
    turned = jnp.stack(
        [cos_rows * real_part - sin_rows * imag_part, cos_rows * imag_part + sin_rows * real_part],
        axis=3,
    ).astype(jnp.bfloat16)
    left = turned.reshape(lags_dev, chans, seg_total * 2 * BINS)
    return jnp.einsum("lik,jk->lij", left, every, preferred_element_type=jnp.float32).astype(
        jnp.bfloat16
    )


NEAREST = ((0, 1, 2, 3), (1, 2, 0, 3), (2, 1, 3, 0), (3, 2, 1, 0))
MESH = pl.DeviceIdType.MESH


def kernel(x_ref, use_ref, line_ref, dft_ref, tab_ref, out_ref, slabs, left, acc, done, sent, got, outs):
    segs, chans, seglen = x_ref.shape
    width = 2 * BINS
    depth = segs * width
    lags = left.shape[1]
    half = chans // 2
    b, z = lax.axis_index("blk"), lax.axis_index("tm")
    core = lax.rem(b, 2)
    at_x = lax.rem(lax.div(b, 2), 2)
    at_y = lax.div(b, 4)
    sib = b + 1 - 2 * core
    by_x = b + 2 - 4 * at_x
    by_y = b + 4 - 8 * at_y
    across = by_x + 4 - 8 * at_y
    up, down = z + 1, z - 1
    has_up, has_down = z < 3, z > 0

    barrier = pltpu.get_barrier_semaphore()
    for peer in (sib, by_x, by_y):
        pl.semaphore_signal(barrier, inc=1, device_id=(peer, z), device_id_type=MESH)

    @pl.when(has_up)
    def _():
        pl.semaphore_signal(barrier, inc=1, device_id=(b, up), device_id_type=MESH)

    @pl.when(has_down)
    def _():
        pl.semaphore_signal(barrier, inc=1, device_id=(b, down), device_id_type=MESH)

    def slab_of(plane, block):
        return plane * 8 + block

    own = slab_of(z, b)
    line = jnp.broadcast_to(line_ref[...], (seglen, 2 * seglen))
    fir = pltpu.roll(line, 0, 1, stride=1, stride_axis=0)[:, :seglen].astype(jnp.bfloat16)
    parts = jnp.dot(fir, dft_ref[...], preferred_element_type=jnp.float32)
    table = (parts[:, :width] + (parts[:, width : 2 * width] + parts[:, 2 * width :])).astype(jnp.bfloat16)
    source = lax.broadcasted_iota(jnp.int32, (seglen, seglen), 0)
    target = lax.broadcasted_iota(jnp.int32, (seglen, seglen), 1)
    band_ones = jnp.where(jnp.abs(source - target) <= SMOOTH, 1.0, 0.0).astype(jnp.bfloat16)
    where = lax.broadcasted_iota(jnp.int32, (1, seglen), 1)
    counts = jnp.minimum(where, SMOOTH) + jnp.minimum(seglen - 1 - where, SMOOTH) + 1
    counts = counts.astype(jnp.float32)
    def whiten_segment(s):
        samples = x_ref[s]
        envelope = jnp.dot(jnp.abs(samples), band_ones, preferred_element_type=jnp.float32) / counts
        normal = (samples.astype(jnp.float32) / (envelope + 1e-06)).astype(jnp.bfloat16)
        spectra = jnp.dot(normal, table, preferred_element_type=jnp.float32)
        power = jnp.sum(spectra * spectra, axis=1, keepdims=True) * jnp.float32(1.0 / BINS)
        scale = use_ref[:, s : s + 1] / jnp.sqrt(power + 1e-06)
        slabs[own, :, s * width : (s + 1) * width] = (spectra * scale).astype(jnp.bfloat16)

    sends = {}

    def view(slab, part):
        if part is None:
            return slabs.at[slab], got.at[slab, 0]
        if part >= 2:
            columns = pl.ds((part - 2) * depth // 2, depth // 2)
            return slabs.at[slab, :, columns], got.at[slab, 0]
        return slabs.at[slab, pl.ds(part * half, half)], got.at[slab, part]

    def make(index, slab, block, plane, part):
        ref, sem = view(slab, part)
        return pltpu.make_async_remote_copy(
            src_ref=ref, dst_ref=ref, send_sem=sent.at[index], recv_sem=sem,
            device_id=(block, plane), device_id_type=MESH,
        )

    def send(name, slab, block, plane, part=None, when=None):
        if name not in sends:
            sends[name] = (len(sends), slab, block, plane, part, when)
        go = make(*sends[name][:-1]).start
        if when is None:
            go()
        else:
            pl.when(when)(go)

    def arrive(slab, part=None):
        make(0, slab, sib, z, part).wait_recv()

    plane_at, onward, goes_on = [z], [None], [None]
    for step in range(1, 4):
        plane = sum(jnp.where(z == at, NEAREST[at][step], 0) for at in range(4))
        following = jnp.where(plane > z, z - 1, z + 1)
        plane_at.append(plane)
        onward.append(following)
        goes_on.append(jnp.logical_and(following >= 0, following <= 3))

    def turn(step):
        slab = slab_of(plane_at[step], b)

        def one(lag, carry):
            row = z * lags + lag
            cos_row = tab_ref[0, pl.ds(row, 1), :]
            sin_row = tab_ref[1, pl.ds(row, 1), :]
            for s in range(segs):
                at = s * width
                real_part = slabs[slab, :, at : at + BINS].astype(jnp.float32)
                imag_part = slabs[slab, :, at + BINS : at + width].astype(jnp.float32)
                left[step, lag, :, at : at + BINS] = (
                    cos_row * real_part - sin_row * imag_part
                ).astype(jnp.bfloat16)
                left[step, lag, :, at + BINS : at + width] = (
                    cos_row * imag_part + sin_row * real_part
                ).astype(jnp.bfloat16)
            return carry

        lax.fori_loop(0, lags, one, 0)

    copies = []

    def correlate(step, block):
        pair = lax.div(block, 2)
        first_slab = slab_of(plane_at[step], pair * 2)
        columns = pl.ds(pl.multiple_of(pair * 2 * chans, 2 * chans), 2 * chans)

        right = slabs[pl.ds(first_slab, 2)].reshape(2 * chans, depth)

        def one(at, carry):
            some = pl.ds(at * GROUP, GROUP)
            term = lax.dot_general(
                left[step, some].reshape(GROUP * chans, depth),
                right,
                (((1,), (1,)), ((), ())),
                preferred_element_type=jnp.float32,
            ).reshape(GROUP, chans, 2 * chans)
            if step == 0:
                acc[some, :, columns] = term
            elif step < 3:
                acc[some, :, columns] += term
            else:
                done[some, :, columns] = (acc[some, :, columns] + term).astype(jnp.bfloat16)
            return carry

        lax.fori_loop(0, lags // GROUP, one, 0)
        if step == 3:
            copy = pltpu.make_async_copy(
                done.at[:, :, columns], out_ref.at[:, :, columns], outs.at[len(copies)]
            )
            copy.start()
            copies.append(copy)

    def other_core(block):
        return block + 1 - 2 * core

    in_middle = jnp.logical_and(has_up, has_down)
    at_end = jnp.logical_not(in_middle)
    mine, xs, ys, corners = [
        [slab_of(plane, block) for plane in plane_at] for block in (b, by_x, by_y, across)
    ]
    twins = {
        key: [slab_of(plane, other_core(block)) for plane in plane_at]
        for key, block in (("b", b), ("x", by_x), ("y", by_y), ("c", across))
    }

    def guarded(when, action):
        if when is None:
            action()
        else:
            pl.when(when)(action)

    def along_z(step, when=None):
        def action():
            slab = mine[step]
            arrive(slab)
            send(("z", step), slab, b, onward[step], when=goes_on[step])
            send(("x", step), slab, by_x, z)
            send(("y", step), slab, by_y, z)
            send(("s", step), slab, sib, z)

        guarded(when, action)

    def neighbours(step):
        arrive(xs[step])
        if step in (0, 3):
            send(("xy", step), xs[step], by_y, z, part=0)
        send(("xs", step), xs[step], sib, z)
        arrive(ys[step])
        if step in (0, 3):
            send(("yx", step), ys[step], by_x, z, part=1)
        send(("ys", step), ys[step], sib, z)

    def corner(step, when=None):
        def action():
            slab = corners[step]
            if step in (0, 3):
                arrive(slab, 0)
                arrive(slab, 1)
            else:
                arrive(slab)
            if step == 0:
                send(("cu",), slab, b, up, when=has_up)
                send(("cd",), slab, b, down, when=has_down)
            elif step == 1:
                send(("cz",), slab, b, onward[1], when=goes_on[1])
            send(("cs", step), slab, sib, z)

        guarded(when, action)

    def multiply(step, keys):
        for key in keys:
            arrive(twins[key][step])
            correlate(step, {"b": b, "x": by_x, "y": by_y, "c": across}[key])

    for part in range(2):
        for segment in range(part * segs // 2, (part + 1) * segs // 2):
            whiten_segment(segment)
        if part == 0:
            pl.semaphore_wait(barrier, 3 + has_up.astype(jnp.int32) + has_down.astype(jnp.int32))
        early = 2 + part
        send(("u", part), own, b, up, early, has_up)
        send(("d", part), own, b, down, early, has_down)
        send(("x", 0, part), own, by_x, z, early)
        send(("y", 0, part), own, by_y, z, early)
        send(("s", 0, part), own, sib, z, early)
    turn(0)
    multiply(0, "b")
    along_z(1)
    along_z(2, in_middle)
    neighbours(0)
    turn(1)
    multiply(0, "xy")
    multiply(1, "b")
    along_z(2, at_end)
    along_z(3, in_middle)
    corner(0)
    turn(2)
    multiply(0, "c")
    neighbours(1)
    along_z(3, at_end)
    corner(1, in_middle)
    multiply(1, "xy")
    multiply(2, "b")
    neighbours(2)
    turn(3)
    multiply(2, "xy")
    multiply(3, "b")
    corner(1, at_end)
    multiply(1, "c")
    neighbours(3)
    multiply(3, "xy")
    corner(2)
    multiply(2, "c")
    corner(3)
    multiply(3, "c")

    for copy in copies:
        copy.wait()
    for index, slab, block, plane, part, when in sends.values():
        guarded(when, make(index, slab, block, plane, part).wait_send)


def kernel_body(records, glitch_mask, fir_taps):
    blocks, planes = lax.axis_size("blk"), lax.axis_size("tm")
    tm_index = lax.axis_index("tm")
    chans, segs, seglen = records.shape
    seg_total = glitch_mask.shape[1]
    lags_dev = LAGS // planes
    depth = segs * 2 * BINS
    usable = lax.dynamic_slice_in_dim(glitch_mask, tm_index * segs, segs, 1).astype(jnp.float32)
    middle = (fir_taps.shape[0] - 1) // 2
    back = fir_taps[::-1].astype(jnp.float32)
    line = jnp.concatenate(
        [back[middle:], jnp.zeros((2 * seglen - 2 * middle - 1,), jnp.float32), back[:middle]]
    )[None, :]
    bf16 = jnp.bfloat16
    return pl.pallas_call(
        kernel,
        out_shape=jax.ShapeDtypeStruct((lags_dev, chans, chans * blocks), bf16),
        in_specs=[pl.BlockSpec(memory_space=pltpu.VMEM)] * 5,
        out_specs=pl.BlockSpec(memory_space=pl.ANY),
        scratch_shapes=[
            pltpu.VMEM((blocks * planes, chans, depth), bf16),
            pltpu.VMEM((planes, lags_dev, chans, depth), bf16),
            pltpu.VMEM((lags_dev, chans, chans * blocks), jnp.float32),
            pltpu.VMEM((lags_dev, chans, chans * blocks), bf16),
            pltpu.SemaphoreType.DMA((48,)),
            pltpu.SemaphoreType.DMA((blocks * planes, 2)),
            pltpu.SemaphoreType.DMA((4,)),
        ],
        compiler_params=pltpu.CompilerParams(
            collective_id=0, has_side_effects=True, vmem_limit_bytes=58 * 1024 * 1024
        ),
        cost_estimate=pl.CostEstimate(
            flops=2 * lags_dev * chans * chans * blocks * planes * depth,
            bytes_accessed=2 * lags_dev * chans * chans * blocks,
            transcendentals=0,
        ),
    )(
        jnp.transpose(records, (1, 0, 2)),
        usable,
        line,
        jnp.asarray(dft_thirds(seglen)),
        jnp.asarray(lag_rows(seg_total, seglen)),
    )


def solution(mesh):
    placed = (P("blk", "tm", None), P("blk", None), P())
    small = mesh.shape["blk"] == 8 and mesh.shape["tm"] == 4
    return jax.shard_map(
        kernel_body if small else gathered_body,
        mesh=mesh,
        in_specs=placed,
        out_specs=P("tm", "blk", None),
        check_vma=False,
    )
```
